256 devices in a mesh: dp: 32 (over z_lo, y, core), tensor: 8 (over z_hi, x).
Axes of the slice: x: 4, y: 4, z: 8 (z_hi: 2, z_lo: 4; z = z_hi * 4 + z_lo), core: 2. Of those that a mesh axis runs over, the one named last changes fastest.
Arguments:
- tokens: bfloat16 [12288, 2560], P(('dp', 'tensor')), may hold values from -24 to 24
- cotangent: bfloat16 [12288, 2560], P(('dp', 'tensor')), may hold values from -1280 to 1280
- gate_pre: bfloat16 [12288, 9216], P('dp', 'tensor'), may hold values from -8 to 8
- up_pre: bfloat16 [12288, 9216], P('dp', 'tensor'), may hold values from -6 to 6
- down_weight: bfloat16 [2560, 9216], P('dp', 'tensor'), may hold values from -0.0625 to 0.0625
- counts: int32 [32, 8], P('dp'), may hold values from 8 to 48, as said below
Outputs:
- grad_gate: float32 [2560, 9216], P('dp', 'tensor')
- grad_up: float32 [2560, 9216], P('dp', 'tensor')
The draws below stay inside these ranges and needn't reach their ends.
Inputs may be any that keep to these rules, and one draw needn't show every extreme that they name: `counts`: every count is a multiple of 8.
All inputs are finite; a program needn't handle non-finite values.
Results may differ from the reference program's by a relative error of at most 0.0029.
Values may be sent and summed in bfloat16 or wider, within the bound.
No kernel may reach another device: no remote copies, remote signals or barrier semaphores. Data moves between devices by JAX's collectives and lax.ppermute only.
A program may use at most 128 MiB of HBM per device.

```python
import jax
import jax.numpy as jnp
from jax import lax

D = 2560
FF = 9216
MB_SLOTS = 48
MICRO = 8
TOKENS = 12288
N_DP = 32


def draw_counts(key, part):
    key = jax.random.fold_in(key, 11)
    levels = MB_SLOTS // 8
    replica = jnp.arange(N_DP, dtype=jnp.int32)[:, None]
    base = 1 + (levels - 2) * replica // max(N_DP - 1, 1)
    extra = jax.random.randint(key, (N_DP, MICRO), 0, 2, dtype=jnp.int32)
    counts = 8 * (base + extra)
    counts = counts.at[N_DP - 1, 0].set(MB_SLOTS)
    counts = counts.at[0, 0].set(8)
    return counts.astype(jnp.int32)


def strengthened(values, rng, source, target, shards_of, factor):
    def block_of(position):
        return (jnp.arange(values.shape[position]) // (values.shape[position] // shards_of)).reshape((-1,) + (1,) * (values.ndim - 1 - position))

    near = jax.random.permutation(rng, shards_of)[block_of(target)]
    far = (block_of(target) + shards_of // 2) % shards_of
    return jnp.where((block_of(source) == near) | (block_of(source) == far), factor * values, values)


def shard_levels(key, shape, cuts, low, top_value):
    level = 1.0
    for dim, shards_of in cuts:
        heights = jax.random.uniform(jax.random.fold_in(jax.random.fold_in(key, 6), dim), (shards_of,), jnp.float32, low / len(cuts), top_value / len(cuts))
        level = level * jnp.repeat(jnp.exp(heights), shape[dim] // shards_of).reshape((-1,) + (1,) * (len(shape) - 1 - dim))
    return level


def noise(key, shape, width, most, cuts=(), held_as=jnp.bfloat16):
    entries = jax.random.normal(key, shape, jnp.float32) * width
    if len(cuts) > 0:
        entries = shard_levels(key, shape, cuts, -0.22, 0.18) * entries
    return jnp.clip(entries, min=-most, max=most).astype(held_as)


def bell_draw_with(own_key, dims, scale, limit, split, heavy, kind=jnp.bfloat16):
    array = scale * jax.random.normal(own_key, dims, jnp.float32)
    if split:
        array = array * shard_levels(own_key, dims, split, -0.22, 0.18)
    return jnp.clip(strengthened(array, jax.random.fold_in(own_key, 3), *heavy), -limit, limit).astype(kind)


def setup_inputs(seed: int = 0) -> dict:
    key_of = jax.random.split(jax.random.key(seed), 7)
    return {
        "tokens": bell_draw_with(key_of[0], (TOKENS, D), 1.0, 24.0, ((0, 256),), (0, 1, 256, 6.0)),
        "cotangent": bell_draw_with(key_of[1], (TOKENS, D), ((MICRO * MB_SLOTS * N_DP) ** 0.5 / 2), 1280.0, ((0, 256),), (0, 1, 256, 6.0)),
        "gate_pre": noise(key_of[2], (TOKENS, FF), 1.5, 8.0, ((0, 32), (1, 8))),
        "up_pre": noise(key_of[3], (TOKENS, FF), 1.0, 6.0, ((0, 32), (1, 8))),
        "down_weight": noise(key_of[4], (D, FF), FF ** -0.5, 0.0625, ((0, 32), (1, 8))),
        "counts": draw_counts(jax.random.fold_in(key_of[6], 71), 0),
    }


def rows_product(left, right, inverse):
    product = lax.dot_general(left, right, (((0,), (0,)), ((), ())), preferred_element_type=jnp.float32)
    return product * inverse


def reference(tokens, cotangent, gate_pre, up_pre, down_weight, counts):
    total = jnp.sum(counts.astype(jnp.float32))
    inverse = 1.0 / total
    slot_index = jnp.arange(MB_SLOTS, dtype=jnp.int32)
    valid_slot = (slot_index[None, None, :] < counts[:, :, None]).reshape(TOKENS)
    masked = jnp.where(valid_slot[:, None], cotangent, jnp.zeros_like(cotangent))
    hidden_grad = lax.dot_general(masked, down_weight, (((1,), (0,)), ((), ())), preferred_element_type=jnp.float32)
    gate_value = gate_pre.astype(jnp.float32)
    up_value = up_pre.astype(jnp.float32)
    sigmoid_gate = jax.nn.sigmoid(gate_value)
    gate_delta = (hidden_grad * up_value * sigmoid_gate * (1.0 + gate_value * (1.0 - sigmoid_gate))).astype(jnp.bfloat16)
    up_delta = (hidden_grad * gate_value * sigmoid_gate).astype(jnp.bfloat16)
    replica_rows = MICRO * MB_SLOTS

    def one_replica(sums, replica):
        begin = (replica * replica_rows).astype(jnp.int32)
        token_block = lax.dynamic_slice_in_dim(tokens, begin, replica_rows, 0)
        gate_block = lax.dynamic_slice_in_dim(gate_delta, begin, replica_rows, 0)
        up_block = lax.dynamic_slice_in_dim(up_delta, begin, replica_rows, 0)
        new_gate = sums[0] + rows_product(token_block, gate_block, inverse)
        new_up = sums[1] + rows_product(token_block, up_block, inverse)
        return (new_gate, new_up), None

    zeros = jnp.zeros((D, FF), jnp.float32)
    sums, unused = lax.scan(one_replica, (zeros, zeros), jnp.arange(N_DP, dtype=jnp.int32))
    return sums[0], sums[1]
```

```python
import jax
import jax.numpy as jnp
from jax import lax
from jax.experimental import pallas as pl
from jax.experimental.pallas import tpu as pltpu
from jax.sharding import PartitionSpec as P

NZ, NY, NC, NW, NX = 4, 4, 2, 2, 4
SLOTS = 48
BLK = 80
D = BLK * NZ * NY * NC
HALF = D // 2
QUART = D // 4
FF = 1152
ROWS = SLOTS * NW * NX
bf16, f32 = jnp.bfloat16, jnp.float32
def dp_move(x, fn):
    pairs = []
    for z in range(NZ):
        for y in range(NY):
            for c in range(NC):
                tz, ty, tc = fn(z, y, c)
                pairs.append(((z * NY + y) * NC + c, (tz * NY + ty) * NC + tc))
    return lax.ppermute(x, "dp", pairs)


def tp_move(x, fn):
    pairs = []
    for w in range(NW):
        for k in range(NX):
            tw, tk = fn(w, k)
            pairs.append((w * NX + k, tw * NX + tk))
    return lax.ppermute(x, "tensor", pairs)


def GATE_PAIR(z, y, c):
    return z, y ^ 1, c


def UP_PAIR(z, y, c):
    return z, 3 - y, c


def core_swap(x):
    return dp_move(x, lambda z, y, c: (z, y, 1 - c))


def vmem():
    return pl.BlockSpec(memory_space=pltpu.VMEM)


def smem():
    return pl.BlockSpec(memory_space=pltpu.SMEM)


def call(body, out_shape, n_smem, n_vmem, scratch=(), flops=0, nbytes=0, mb=40):
    return pl.pallas_call(
        body,
        out_shape=out_shape,
        in_specs=[smem()] * n_smem + [vmem()] * n_vmem,
        out_specs=jax.tree.map(lambda _: vmem(), out_shape),
        scratch_shapes=list(scratch),
        compiler_params=pltpu.CompilerParams(vmem_limit_bytes=mb << 20),
        cost_estimate=pl.CostEstimate(flops=flops, bytes_accessed=nbytes, transcendentals=0),
    )


def sds(shape, dtype):
    return jax.ShapeDtypeStruct(shape, dtype)


def columns(x, chosen):
    return jnp.concatenate([x[:, i * BLK : (i + 1) * BLK] for i in chosen], axis=1)


def half_blocks(core):
    return [chip * NC + core for chip in range(NZ * NY)]


def split_body(pos, counts, cot, tok, keep, send):
    live = counts[0, pos[3] * NX + pos[4]]
    row = lax.broadcasted_iota(jnp.int32, (SLOTS, 1), 0)
    first = pos[2] == 0
    cot_rows = jnp.where(row < live, cot[...].astype(f32), 0.0)
    for at, x in ((0, cot_rows), (SLOTS, tok[...].astype(f32))):
        even, odd = columns(x, half_blocks(0)), columns(x, half_blocks(1))
        keep[at : at + SLOTS, :] = jnp.where(first, even, odd).astype(bf16)
        send[at : at + SLOTS, :] = jnp.where(first, odd, even).astype(bf16)
    total = counts[0, 0]
    for m in range(1, 8):
        total += counts[0, m]
    eighths = jnp.full((16, HALF), lax.div(total, 8), jnp.int32).astype(bf16)
    keep[2 * SLOTS :, :] = eighths
    send[2 * SLOTS :, :] = eighths


def join_body(pos, keep, recv, cot, gate_keep, gate_send, up_keep, up_send):
    cot[:SLOTS, :] = keep[:SLOTS, :]
    cot[SLOTS:, :] = recv[:SLOTS, :]
    x = jnp.concatenate([keep[SLOTS : 2 * SLOTS, :], recv[SLOTS : 2 * SLOTS, :]], axis=0).astype(f32)
    of_y = [columns(x, [z * NY + y for z in range(NZ)]) for y in range(NY)]
    n = (keep[2 * SLOTS :, :QUART].astype(f32) + recv[2 * SLOTS :, :QUART].astype(f32)).astype(bf16)

    def pick(y):
        low = jnp.where(y == 0, of_y[0], of_y[1])
        return jnp.where(y < 2, low, jnp.where(y == 2, of_y[2], of_y[3]))

    y = pos[1]
    even = lax.rem(y, 2) == 0
    mine, flip = pick(y), pick(jnp.where(even, y + 1, y - 1))
    back, both = pick(3 - y), pick(3 - jnp.where(even, y + 1, y - 1))
    for out, l, r in (
        (gate_keep, mine, back),
        (gate_send, flip, both),
        (up_keep, mine, flip),
        (up_send, back, both),
    ):
        out[: 2 * SLOTS, :] = jnp.concatenate([l, r], axis=1).astype(bf16)
    gate_keep[2 * SLOTS :, :] = n
    gate_send[2 * SLOTS :, :] = n


def tok_body(gate_keep, gate_recv, up_keep, up_recv, tok, eighths):
    h = 2 * SLOTS
    for i, piece in enumerate((gate_keep, gate_recv, up_keep, up_recv)):
        tok[i * h : (i + 1) * h, :] = piece[:h, :]
    eighths[...] = gate_keep[h:, :128].astype(f32) + gate_recv[h:, :128].astype(f32)


def sets_body(tok, far, gate, up):
    h = 4 * SLOTS
    for i, piece in enumerate((tok, far)):
        gate[i * h : (i + 1) * h, :] = piece[:h, :]
        up[i * h : (i + 1) * h, :] = piece[h:, :]


def put_count(send, at, n):
    high = jnp.floor(n * (1.0 / 32.0))
    send[at:, :] = jnp.zeros((16, FF), bf16)
    send[at:, :128] = high.astype(bf16)
    send[at:, 128:256] = (n - 32.0 * high).astype(bf16)


def get_count(recv, at):
    return 32.0 * recv[at:, :128].astype(f32) + recv[at:, 128:256].astype(f32)


T_SHIFTS = [(dw, dx) for dw in range(NW) for dx in range(NX)]


def tensor_slot(pos, dw, dx):
    return lax.rem(pos[3] + dw, NW) * NX + lax.rem(pos[4] - dx + NX, NX)


def rows_of(pieces, d, at, count):
    mine, left, right, top, bottom = pieces
    half = top.shape[0]
    if d == 2:
        return top[at : at + count, :] if at < half else bottom[at - half : at - half + count, :]
    return (mine, left, None, right)[d][at : at + count, :]


def hidden_body(pos, *refs):
    cots, weights = refs[:5], refs[5:10]
    own, other, a, b = refs[10:]
    for dx in range(NX):
        for dw in range(NW):
            at = pl.multiple_of(tensor_slot(pos, dw, dx) * SLOTS, 16)
            for i in range(2):
                a[pl.ds(at + i * ROWS, SLOTS), :] = rows_of(cots, dx, (dw * 2 + i) * SLOTS, SLOTS)
    for dy in range(NY):
        y = lax.rem(pos[1] - dy + NY, NY)
        for dz in range(NZ):
            z = lax.rem(pos[0] - dz + NZ, NZ)
            to = pl.multiple_of((z * NY + y) * BLK, 16)
            b[pl.ds(to, BLK), :] = rows_of(weights, dy, dz * BLK, BLK)
    for part, out in ((1, other), (0, own)):
        for n in range(0, FF, 384):
            out[:, n : n + 384] = jnp.dot(
                a[part * ROWS : (part + 1) * ROWS, :], b[:, n : n + 384], preferred_element_type=f32
            )


def delta_body(own, recv, gate_pre, up_pre, gate_delta, up_delta, both):
    def step(i, carry):
        at = pl.ds(pl.multiple_of(i * 48, 16), 48)
        h = own[at, :] + recv[at, :]
        g, u = gate_pre[at, :].astype(f32), up_pre[at, :].astype(f32)
        sg = 1.0 / (1.0 + jnp.exp(-g))
        hs = h * sg
        gate_delta[at, :] = (hs * u * (1.0 + g * (1.0 - sg))).astype(bf16)
        up_delta[at, :] = (hs * g).astype(bf16)
        both[at, :] = gate_delta[at, :]
        both[pl.ds(pl.multiple_of(ROWS + i * 48, 16), 48), :] = up_delta[at, :]
        return carry

    lax.fori_loop(0, ROWS // 48, step, 0)


def turn_body(pos, *refs):
    pieces, (xt, x) = refs[:5], refs[5:]
    for dx in range(NX):
        for dw in range(NW):
            at = tensor_slot(pos, dw, dx) * SLOTS
            for s in range(4):
                to = pl.multiple_of(at + s * ROWS, 16)
                x[pl.ds(to, SLOTS), :] = rows_of(pieces, dx, (dw * 4 + s) * SLOTS, SLOTS)
    for a in range(0, 4 * ROWS, 128):
        xt[:, a : a + 128] = x[a : a + 128, :].T


def grad_part(xt, deltas, keep, send):
    for part, out in ((1, send), (0, keep)):
        for n in range(0, FF, 384):
            acc = None
            for s, d in enumerate(deltas):
                term = jnp.dot(
                    xt[part * 320 : (part + 1) * 320, s * ROWS : (s + 1) * ROWS],
                    d[:, n : n + 384],
                    preferred_element_type=f32,
                )
                acc = term if acc is None else acc + term
            out[:320, n : n + 384] = acc.astype(out.dtype)


def gate_grad_body(xt, d0, d1, d2, d3, eighths, keep, send):
    grad_part(xt, (d0, d1.at[:ROWS], d2, d3), keep, send)
    put_count(send, 320, eighths[...])


def up_grad_body(xt, d0, d1, d2, d3, keep, send):
    grad_part(xt, (d0, d1.at[ROWS:], d2, d3), keep, send)


def ysum(pos, keep, recv, own, send):
    z = pos[0]
    z1 = jnp.where(lax.rem(z, 2) == 0, z + 1, z - 1)
    for out, first in ((send, z1), (own, z)):
        for half, block in ((0, first), (1, lax.rem(first + 2, NZ))):
            at = pl.ds(pl.multiple_of(block * BLK, 16), BLK)
            out[half * BLK : (half + 1) * BLK, :] = (keep[at, :] + recv[at, :].astype(f32)).astype(out.dtype)


def gate_ysum_body(pos, keep, recv, n, own, send, n_out):
    ysum(pos, keep, recv, own, send)
    n_out[...] = n[...] + get_count(recv, 320)
    put_count(send, 2 * BLK, n_out[...])


def up_ysum_body(pos, keep, recv, own, send):
    ysum(pos, keep, recv, own, send)


def zsum(keep, recv, own, send):
    send[:BLK, :] = (keep[BLK:, :] + recv[BLK : 2 * BLK, :].astype(f32)).astype(bf16)
    own[...] = keep[:BLK, :] + recv[:BLK, :].astype(f32)


def gate_zsum_body(keep, recv, n, own, send, n_out):
    zsum(keep, recv, own, send)
    n_out[...] = n[...] + get_count(recv, 2 * BLK)
    put_count(send, BLK, n_out[...])


def up_zsum_body(keep, recv, own, send):
    zsum(keep, recv, own, send)


def gate_final_body(own, recv, n, out, inverse):
    total = 8.0 * (n[...] + get_count(recv, BLK))
    inverse[...] = 1.0 / total
    out[...] = (own[...] + recv[:BLK, :].astype(f32)) * inverse[0:1, 0:1]


def up_final_body(own, recv, inverse, out):
    out[...] = (own[...] + recv[...].astype(f32)) * inverse[0:1, 0:1]


def x_move(x, d):
    return tp_move(x, lambda w, k: (w, (k + d) % NX))


def y_move(x, d):
    return dp_move(x, lambda z, y, c: (z, (y + d) % NY, c))


def ring(x, move):
    half = x.shape[0] // 2
    left, right = move(x, 1), move(x, -1)
    return x, left, right, move(left[:half], 1), move(right[half:], -1)


def w_move(x):
    return tp_move(x, lambda w, k: (1 - w, k))


def after(x, *others):
    return lax.optimization_barrier((x, *others))[0]


def local(tokens, cotangent, gate_pre, up_pre, down_weight, counts):
    dp, tp = lax.axis_index("dp"), lax.axis_index("tensor")
    pos = jnp.stack([dp // 8, dp // 2 % 4, dp % 2, tp // 4, tp % 4]).astype(jnp.int32)

    w_z = [dp_move(down_weight, lambda z, y, c: ((z + dz) % NZ, y, c)) for dz in (1, 2, 3)]
    both = sds((2 * SLOTS + 16, HALF), bf16)
    keep, send = call(split_body, (both, both), 2, 2)(pos, counts, cotangent, tokens)
    quart = sds((2 * SLOTS, QUART), bf16)
    quart_n = sds((2 * SLOTS + 16, QUART), bf16)
    cot, gate_keep, gate_send, up_keep, up_send = call(
        join_body, (sds((2 * SLOTS, HALF), bf16), quart_n, quart_n, quart, quart), 1, 2
    )(pos, keep, core_swap(send))
    far = w_move(cot)
    cots = ring(jnp.concatenate([cot, far], axis=0), x_move)
    gate_recv = dp_move(gate_send, GATE_PAIR)
    up_recv = dp_move(up_send, UP_PAIR)
    tok, eighths = call(tok_body, (sds((8 * SLOTS, QUART), bf16), sds((16, 128), f32)), 0, 4)(
        gate_keep, gate_recv, up_keep, up_recv
    )
    w_z, tok = lax.optimization_barrier((w_z, tok))
    weights = ring(jnp.concatenate([down_weight, *w_z], axis=0), y_move)
    tok_far = w_move(after(tok, far))
    tset = sds((8 * SLOTS, QUART), bf16)
    gate_set, up_set = call(sets_body, (tset, tset), 0, 2)(tok, tok_far)
    gate_toks = ring(after(gate_set, *cots), x_move)
    up_toks = ring(after(up_set, *gate_toks), x_move)

    weights = lax.optimization_barrier((*weights, gate_set))[:5]
    hid = sds((ROWS, FF), f32)
    own, other = call(
        hidden_body,
        (hid, hid),
        1,
        10,
        [pltpu.VMEM((2 * ROWS, HALF), bf16), pltpu.VMEM((HALF, FF), bf16)],
        flops=2 * 2 * ROWS * HALF * FF,
        nbytes=8 << 20,
    )(pos, *cots, *weights)
    recv = core_swap(other)
    delta = sds((ROWS, FF), bf16)
    gate_delta, up_delta, both = call(delta_body, (delta, delta, sds((2 * ROWS, FF), bf16)), 0, 4, nbytes=6 << 20)(
        own, recv, gate_pre, up_pre
    )

    xt = sds((QUART, 4 * ROWS), bf16)
    turn = call(turn_body, xt, 1, 5, [pltpu.VMEM((4 * ROWS, QUART), bf16)])
    cost = dict(flops=2 * 4 * ROWS * QUART * FF, nbytes=8 << 20)
    n = sds((16, 128), f32)

    e = dp_move(gate_delta, GATE_PAIR)
    f = dp_move(up_delta, UP_PAIR)
    other = core_swap(both)
    gate = (gate_delta, other, e, core_swap(e))
    up = (up_delta, other, f, core_swap(f))

    def z1(x):
        return dp_move(x, lambda z, y, c: (z ^ 1, y, c))

    def z2(x):
        return dp_move(x, lambda z, y, c: (z ^ 2, y, c))

    keep, send = call(gate_grad_body, (sds((320, FF), f32), sds((336, FF), bf16)), 0, 6, **cost)(
        turn(pos, *gate_toks), *gate, eighths
    )
    got = dp_move(send, UP_PAIR)
    keep, send, eighths = call(gate_ysum_body, (sds((2 * BLK, FF), f32), sds((2 * BLK + 16, FF), bf16), n), 1, 3)(
        pos, keep, got, eighths
    )
    got = z1(send)
    keep, send, eighths = call(gate_zsum_body, (sds((BLK, FF), f32), sds((BLK + 16, FF), bf16), n), 0, 3)(
        keep, got, eighths
    )
    grad_gate, inverse = call(gate_final_body, (sds((BLK, FF), f32), n), 0, 3)(keep, z2(send), eighths)

    keep, send = call(up_grad_body, (sds((320, FF), f32), sds((320, FF), bf16)), 0, 5, **cost)(
        turn(pos, *up_toks), *up
    )
    got = dp_move(send, GATE_PAIR)
    keep, send = call(up_ysum_body, (sds((2 * BLK, FF), f32), sds((2 * BLK, FF), bf16)), 1, 2)(pos, keep, got)
    got = z1(send)
    keep, send = call(up_zsum_body, (sds((BLK, FF), f32), sds((BLK, FF), bf16)), 0, 2)(keep, got)
    grad_up = call(up_final_body, sds((BLK, FF), f32), 0, 3)(keep, z2(send), inverse)
    return grad_gate, grad_up


def solution(mesh):
    rows = P(("dp", "tensor"), None)
    both = P("dp", "tensor")
    return jax.shard_map(
        local,
        mesh=mesh,
        in_specs=(rows, rows, both, both, both, P("dp", None)),
        out_specs=(both, both),
        check_vma=False,
    )
```

```python
import jax
import jax.numpy as jnp
from jax import lax
from jax.experimental import pallas as pl
from jax.experimental.pallas import tpu as pltpu
from jax.sharding import PartitionSpec as P

NZ, NY, NC, NW, NX = 4, 4, 2, 2, 4
SLOTS = 48
BLK = 80
D = BLK * NZ * NY * NC
HALF = D // 2
QUART = D // 4
FF = 1152
ROWS = SLOTS * NW * NX
bf16, f32 = jnp.bfloat16, jnp.float32
def dp_move(x, fn):
    pairs = []
    for z in range(NZ):
        for y in range(NY):
            for c in range(NC):
                tz, ty, tc = fn(z, y, c)
                pairs.append(((z * NY + y) * NC + c, (tz * NY + ty) * NC + tc))
    return lax.ppermute(x, "dp", pairs)


def tp_move(x, fn):
    pairs = []
    for w in range(NW):
        for k in range(NX):
            tw, tk = fn(w, k)
            pairs.append((w * NX + k, tw * NX + tk))
    return lax.ppermute(x, "tensor", pairs)


def GATE_PAIR(z, y, c):
    return z, y ^ 1, c


def UP_PAIR(z, y, c):
    return z, 3 - y, c


def core_swap(x):
    return dp_move(x, lambda z, y, c: (z, y, 1 - c))


def vmem():
    return pl.BlockSpec(memory_space=pltpu.VMEM)


def smem():
    return pl.BlockSpec(memory_space=pltpu.SMEM)


def call(body, out_shape, n_smem, n_vmem, scratch=(), flops=0, nbytes=0, mb=40):
    return pl.pallas_call(
        body,
        out_shape=out_shape,
        in_specs=[smem()] * n_smem + [vmem()] * n_vmem,
        out_specs=jax.tree.map(lambda _: vmem(), out_shape),
        scratch_shapes=list(scratch),
        compiler_params=pltpu.CompilerParams(vmem_limit_bytes=mb << 20),
        cost_estimate=pl.CostEstimate(flops=flops, bytes_accessed=nbytes, transcendentals=0),
    )


def sds(shape, dtype):
    return jax.ShapeDtypeStruct(shape, dtype)


def columns(x, chosen):
    return jnp.concatenate([x[:, i * BLK : (i + 1) * BLK] for i in chosen], axis=1)


def choose(i, options):
    low = jnp.where(i == 0, options[0], options[1])
    return jnp.where(i < 2, low, jnp.where(i == 2, options[2], options[3]))


def half_blocks(core):
    return [chip * NC + core for chip in range(NZ * NY)]


def split_body(pos, counts, cot, tok, keep, send):
    live = counts[0, pos[3] * NX + pos[4]]
    row = lax.broadcasted_iota(jnp.int32, (SLOTS, 1), 0)
    first = pos[2] == 0
    cot_rows = jnp.where(row < live, cot[...].astype(f32), 0.0)
    for at, x in ((0, cot_rows), (SLOTS, tok[...].astype(f32))):
        even, odd = columns(x, half_blocks(0)), columns(x, half_blocks(1))
        keep[at : at + SLOTS, :] = jnp.where(first, even, odd).astype(bf16)
        send[at : at + SLOTS, :] = jnp.where(first, odd, even).astype(bf16)
    total = counts[0, 0]
    for m in range(1, 8):
        total += counts[0, m]
    eighths = jnp.full((16, HALF), lax.div(total, 8), jnp.int32).astype(bf16)
    keep[2 * SLOTS :, :] = eighths
    send[2 * SLOTS :, :] = eighths


def join_body(pos, keep, recv, cot, gate_keep, gate_send, up_keep, up_send):
    cot[:SLOTS, :] = keep[:SLOTS, :]
    cot[SLOTS:, :] = recv[:SLOTS, :]
    x = jnp.concatenate([keep[SLOTS : 2 * SLOTS, :], recv[SLOTS : 2 * SLOTS, :]], axis=0).astype(f32)
    z_orders = [[z ^ k for k in (1, 3, 0, 2)] for z in range(NZ)]
    of_y = [
        choose(pos[0], [columns(x, [zz * NY + y for zz in order]) for order in z_orders]) for y in range(NY)
    ]
    n = (keep[2 * SLOTS :, :QUART].astype(f32) + recv[2 * SLOTS :, :QUART].astype(f32)).astype(bf16)

    y = pos[1]
    even = lax.rem(y, 2) == 0
    flipped = jnp.where(even, y + 1, y - 1)
    mine, flip, back, both = [choose(at, of_y) for at in (y, flipped, 3 - y, 3 - flipped)]
    for out, l, r in (
        (gate_keep, back, mine),
        (gate_send, both, flip),
        (up_keep, flip, mine),
        (up_send, both, back),
    ):
        out[: 2 * SLOTS, :] = jnp.concatenate([l, r], axis=1).astype(bf16)
    gate_keep[2 * SLOTS :, :] = n
    gate_send[2 * SLOTS :, :] = n


def tok_body(gate_keep, gate_recv, up_keep, up_recv, tok, eighths):
    h = 2 * SLOTS
    for i, piece in enumerate((gate_keep, gate_recv, up_keep, up_recv)):
        tok[i * h : (i + 1) * h, :] = piece[:h, :]
    eighths[...] = gate_keep[h:, :128].astype(f32) + gate_recv[h:, :128].astype(f32)


def slab_body(*refs):
    for i, piece in enumerate(refs[:4]):
        refs[4][i * BLK : (i + 1) * BLK, :] = piece[...]


def relay_body(left, far_left, right, far_right, gate, up):
    h = 4 * SLOTS
    gate[:h, :], gate[h:, :] = left[:h, :], far_left[:h, :]
    up[:h, :], up[h:, :] = right[h:, :], far_right[h:, :]


def put_count(send, at, n):
    high = jnp.floor(n * (1.0 / 32.0))
    send[at:, :] = jnp.zeros((16, FF), bf16)
    send[at:, :128] = high.astype(bf16)
    send[at:, 128:256] = (n - 32.0 * high).astype(bf16)


def get_count(recv, at):
    return 32.0 * recv[at:, :128].astype(f32) + recv[at:, 128:256].astype(f32)


T_SHIFTS = [(dw, dx) for dw in range(NW) for dx in range(NX)]


def tensor_slot(pos, dw, dx):
    return lax.rem(pos[3] + dw, NW) * NX + lax.rem(pos[4] - dx + NX, NX)


def rows_of(pieces, d, at, count):
    mine, left, right, top, bottom = pieces
    half = top.shape[0]
    if d == 2:
        return top[at : at + count, :] if at < half else bottom[at - half : at - half + count, :]
    return (mine, left, None, right)[d][at : at + count, :]


def hidden_body(pos, *refs):
    cots, weights = refs[:5], refs[5:10]
    other, own_rows, b, a = refs[10:]
    for dx in range(NX):
        for dw in range(NW):
            at = pl.multiple_of(tensor_slot(pos, dw, dx) * SLOTS, 16)
            for i, to in enumerate((own_rows, a)):
                to[pl.ds(at, SLOTS), :] = rows_of(cots, dx, (dw * 2 + i) * SLOTS, SLOTS)
    for dy in range(NY):
        y = lax.rem(pos[1] - dy + NY, NY)
        for dz in range(NZ):
            z = pos[0] ^ dz
            to = pl.multiple_of((z * NY + y) * BLK, 16)
            b[pl.ds(to, BLK), :] = rows_of(weights, dy, dz * BLK, BLK)
    product(a, b, other)


def product(a, b, out):
    for n in range(0, FF, 384):
        out[:, n : n + 384] = jnp.dot(a[...], b[:, n : n + 384], preferred_element_type=f32)


def own_body(a, b, out):
    product(a, b, out)


def delta_body(own, recv, gate_pre, up_pre, gate_delta, up_delta, both):
    def step(i, carry):
        at = pl.ds(pl.multiple_of(i * 48, 16), 48)
        h = own[at, :] + recv[at, :]
        g, u = gate_pre[at, :].astype(f32), up_pre[at, :].astype(f32)
        sg = 1.0 / (1.0 + jnp.exp(-g))
        hs = h * sg
        gate_delta[at, :] = (hs * u * (1.0 + g * (1.0 - sg))).astype(bf16)
        up_delta[at, :] = (hs * g).astype(bf16)
        both[at, :] = gate_delta[at, :]
        both[pl.ds(pl.multiple_of(ROWS + i * 48, 16), 48), :] = up_delta[at, :]
        return carry

    lax.fori_loop(0, ROWS // 48, step, 0)


def turn(first, pos, *refs):
    near, far, opposite, xt, x = refs[:3], refs[3:6], refs[6], refs[7], refs[8]
    h = 4 * SLOTS
    for dx in range(NX):
        for dw, pieces in enumerate((near, far)):
            at = tensor_slot(pos, dw, dx) * SLOTS
            piece, base = (opposite, dw * h) if dx == 2 else ((pieces[0], pieces[1], None, pieces[2])[dx], first)
            for s in range(4):
                i = base + s * SLOTS
                x[pl.ds(pl.multiple_of(at + s * ROWS, 16), SLOTS), :] = piece[i : i + SLOTS, :]
    for a in range(0, 4 * ROWS, 128):
        xt[:, a : a + 128] = x[a : a + 128, :].T


def gate_turn_body(pos, *refs):
    turn(0, pos, *refs)


def up_turn_body(pos, *refs):
    turn(4 * SLOTS, pos, *refs)


GROUP = 2 * BLK


def add_product(acc, xt, deltas, first, rows, out):
    for n in range(0, FF, 384):
        total = None if acc is None else acc[rows, n : n + 384]
        for s, d in enumerate(deltas):
            at = (first + s) * ROWS
            term = jnp.dot(xt[rows, at : at + ROWS], d[:, n : n + 384], preferred_element_type=f32)
            total = term if total is None else total + term
        out[: rows.stop - rows.start, n : n + 384] = total.astype(out.dtype)


def gate_near_body(xt, d, other, acc):
    add_product(None, xt, (d, other.at[:ROWS]), 0, slice(0, QUART), acc)


def up_near_body(xt, d, other, acc):
    add_product(None, xt, (d, other.at[ROWS:]), 0, slice(0, QUART), acc)


def far_body(acc, xt, e, e2, send, keep):
    add_product(acc, xt, (e, e2), 2, slice(0, 2 * GROUP), send)
    add_product(acc, xt, (e, e2), 2, slice(2 * GROUP, 4 * GROUP), keep)


def gate_far_body(acc, xt, e, e2, eighths, send, keep):
    far_body(acc, xt, e, e2, send, keep)
    put_count(send, 2 * GROUP, eighths[...])


def z1(keep, recv, send, rest):
    send[:GROUP, :] = (keep[:GROUP, :] + recv[:GROUP, :].astype(f32)).astype(bf16)
    rest[...] = keep[GROUP:, :] + recv[GROUP : 2 * GROUP, :].astype(f32)


def gate_z1_body(keep, recv, n, send, rest, n_out):
    z1(keep, recv, send, rest)
    n_out[...] = n[...] + get_count(recv, 2 * GROUP)
    put_count(send, GROUP, n_out[...])


def up_z1_body(keep, recv, send, rest):
    z1(keep, recv, send, rest)


def z2(part, got, own, send):
    send[:BLK, :] = (part[BLK:, :] + got[BLK : 2 * BLK, :].astype(f32)).astype(bf16)
    own[...] = part[:BLK, :] + got[:BLK, :].astype(f32)


def gate_z2_body(part, got, n, own, send, n_out):
    z2(part, got, own, send)
    n_out[...] = n[...] + get_count(got, GROUP)
    put_count(send, BLK, n_out[...])


def up_z2_body(part, got, own, send):
    z2(part, got, own, send)


def gate_final_body(own, recv, n, out, inverse):
    total = 8.0 * (n[...] + get_count(recv, BLK))
    inverse[...] = 1.0 / total
    out[...] = (own[...] + recv[:BLK, :].astype(f32)) * inverse[0:1, 0:1]


def up_final_body(own, recv, inverse, out):
    out[...] = (own[...] + recv[...].astype(f32)) * inverse[0:1, 0:1]


def x_move(x, d):
    return tp_move(x, lambda w, k: (w, (k + d) % NX))


def y_move(x, d):
    return dp_move(x, lambda z, y, c: (z, (y + d) % NY, c))


def z_move(x, k):
    return dp_move(x, lambda z, y, c: (z ^ k, y, c))


def ring(x, move):
    half = x.shape[0] // 2
    left, right = move(x, 1), move(x, -1)
    return x, left, right, move(left[:half], 1), move(right[half:], -1)


def w_move(x):
    return tp_move(x, lambda w, k: (1 - w, k))


def after(x, *others):
    return lax.optimization_barrier((x, *others))[0]


def local(tokens, cotangent, gate_pre, up_pre, down_weight, counts):
    dp, tp = lax.axis_index("dp"), lax.axis_index("tensor")
    pos = jnp.stack([dp // 8, dp // 2 % 4, dp % 2, tp // 4, tp % 4]).astype(jnp.int32)

    w_z = [z_move(down_weight, k) for k in (1, 2, 3)]
    both = sds((2 * SLOTS + 16, HALF), bf16)
    keep, send = call(split_body, (both, both), 2, 2)(pos, counts, cotangent, tokens)
    quart = sds((2 * SLOTS, QUART), bf16)
    quart_n = sds((2 * SLOTS + 16, QUART), bf16)
    cot, gate_keep, gate_send, up_keep, up_send = call(
        join_body, (sds((2 * SLOTS, HALF), bf16), quart_n, quart_n, quart, quart), 1, 2
    )(pos, keep, core_swap(send))
    far = w_move(cot)
    gate_recv = dp_move(gate_send, GATE_PAIR)
    up_recv = dp_move(up_send, UP_PAIR)
    tok, eighths = call(tok_body, (sds((8 * SLOTS, QUART), bf16), sds((16, 128), f32)), 0, 4)(
        gate_keep, gate_recv, up_keep, up_recv
    )
    near = [tok, x_move(tok, 1), x_move(tok, -1)]
    slab = call(slab_body, sds((NZ * BLK, FF), bf16), 0, 4, flops=20_000_000_000)
    weights = ring(slab(down_weight, *w_z), y_move)
    cots = ring(after(jnp.concatenate([cot, far], axis=0), *near), x_move)
    tok_far = w_move(after(tok, far))
    tok_far_x = after(tok_far, *cots)
    away = [tok_far, x_move(tok_far_x, 1), x_move(tok_far_x, -1)]
    relay = sds((8 * SLOTS, QUART), bf16)
    gate_opposite, up_opposite = call(relay_body, (relay, relay), 0, 4, flops=20_000_000_000)(
        near[1], away[1], near[2], away[2]
    )
    gate_opposite, up_opposite = x_move(gate_opposite, 1), x_move(up_opposite, -1)

    weights = lax.optimization_barrier((*weights, tok_far))[:5]
    hid = sds((ROWS, FF), f32)
    other, own_rows, whole_weight = call(
        hidden_body,
        (hid, sds((ROWS, HALF), bf16), sds((HALF, FF), bf16)),
        1,
        10,
        [pltpu.VMEM((ROWS, HALF), bf16)],
        flops=2 * ROWS * HALF * FF,
        nbytes=8 << 20,
    )(pos, *cots, *weights)
    recv = core_swap(other)
    own = call(own_body, hid, 0, 2, flops=2 * ROWS * HALF * FF, nbytes=8 << 20)(own_rows, whole_weight)
    delta = sds((ROWS, FF), bf16)
    gate_delta, up_delta, both = call(delta_body, (delta, delta, sds((2 * ROWS, FF), bf16)), 0, 4, nbytes=6 << 20)(
        own, recv, gate_pre, up_pre
    )

    other = core_swap(both)
    e = dp_move(gate_delta, GATE_PAIR)
    f = dp_move(up_delta, UP_PAIR)

    xt = sds((QUART, 4 * ROWS), bf16)
    scratch = [pltpu.VMEM((4 * ROWS, QUART), bf16)]
    acc = sds((QUART, FF), f32)
    half = dict(flops=4 * ROWS * QUART * FF, nbytes=6 << 20)
    n = sds((16, 128), f32)
    part, part_n = sds((GROUP, FF), bf16), sds((GROUP + 16, FF), bf16)

    gate_xt = call(gate_turn_body, xt, 1, 7, scratch)(pos, *near, *away, gate_opposite)
    up_xt = call(up_turn_body, xt, 1, 7, scratch)(pos, *near, *away, up_opposite)
    gate_acc = call(gate_near_body, acc, 0, 3, **half)(gate_xt, gate_delta, other)
    up_acc = call(up_near_body, acc, 0, 3, **half)(up_xt, up_delta, other)
    e2, f2 = core_swap(after(e, gate_acc, up_acc)), core_swap(after(f, gate_acc, up_acc))

    kept, last = sds((2 * GROUP, FF), f32), sds((GROUP, FF), f32)
    send, gate_keep = call(gate_far_body, (sds((2 * GROUP + 16, FF), bf16), kept), 0, 5, **half)(
        gate_acc, gate_xt, e, e2, eighths
    )
    gate_got = dp_move(send, UP_PAIR)
    send, up_keep = call(far_body, (sds((2 * GROUP, FF), bf16), kept), 0, 4, **half)(up_acc, up_xt, f, f2)
    up_got = dp_move(send, GATE_PAIR)

    send, gate_keep, eighths = call(gate_z1_body, (part_n, last, n), 0, 3)(gate_keep, gate_got, eighths)
    gate_got = z_move(send, 1)
    send, up_keep = call(up_z1_body, (part, last), 0, 2)(up_keep, after(up_got, send))
    up_got = z_move(send, 1)

    mine = sds((BLK, FF), f32)
    own, send, eighths = call(gate_z2_body, (mine, sds((BLK + 16, FF), bf16), n), 0, 3)(gate_keep, gate_got, eighths)
    grad_gate, inverse = call(gate_final_body, (mine, n), 0, 3)(own, z_move(send, 2), eighths)
    own, send = call(up_z2_body, (mine, sds((BLK, FF), bf16)), 0, 2)(up_keep, up_got)
    grad_up = call(up_final_body, mine, 0, 3)(own, z_move(send, 2), inverse)
    return grad_gate, grad_up


def solution(mesh):
    rows = P(("dp", "tensor"), None)
    both = P("dp", "tensor")
    return jax.shard_map(
        local,
        mesh=mesh,
        in_specs=(rows, rows, both, both, both, P("dp", None)),
        out_specs=(both, both),
        check_vma=False,
    )
```
